32 devices in a mesh: groups: 2 (over y), sector: 4 (over z), chan: 2 (over x), rep: 2 (over core).
Axes of the slice: x: 2, y: 2, z: 4, core: 2. Of those that a mesh axis runs over, the one named last changes fastest.
Arguments:
- theta: bfloat16 [48, 256, 256], P(('groups', 'sector')), parts along dimension 0, may hold values from -6 to 6
- left_env: bfloat16 [12, 24, 256, 256], P(('groups', 'chan'), 'sector', 'rep'), parts along dimension 0, may hold values from -0.375 to 0.375
- right_env: bfloat16 [12, 24, 256, 256], P(('groups', 'chan'), 'sector'), parts along dimension 0, may hold values from -0.375 to 0.375
- coef: float32 [48, 6, 4], P(('groups', 'sector'), 'chan'), parts along dimension 0, may hold values from -0.6 to 0.6
- term_slot: int32 [48, 6, 4], P(('groups', 'sector'), 'chan'), parts along dimension 0, may hold values from 0 to 7, as said below
- need: int32 [8, 4, 2], P('groups'), parts along dimension 0, may hold values from 0 to 5
- dims: int32 [48, 2], P(('groups', 'sector')), parts along dimension 0, may hold values from 64 to 256
Outputs:
- product: float32 [48, 256, 256], P(('groups', 'sector'), 'rep'), parts along dimension 0
The draws below stay inside these ranges and needn't reach their ends.
There are 2 independent parts, one for each index of `groups`. The reference program is written for one: setup_inputs(seed, part) draws one part's arguments, and reference() takes and returns one part's arrays. A program takes and returns all parts, laid end to end along the dimension named above; each array names one. Nothing has to cross between parts.
Inputs may be any that keep to these rules, and one draw needn't show every extreme that they name: `term_slot`: for each owner of 6 blocks and each shard of 3 channels, every slot 0 to 4 * 2 - 1 is named by at least one term.
All inputs are finite; a program needn't handle non-finite values.
Results may differ from the reference program's by a relative error of at most 0.0029.
Values may be sent and summed in bfloat16 or wider, within the bound.
A program may use at most 64 MiB of HBM per device.

```python
import jax
import jax.numpy as jnp
from jax import lax

M = 256
OB = 6
CH_DEV = 3
TPC = 4
CAP = 2
NBLK = 24
CH = 6
N_SECTOR = 4
N_CHAN = 2


def draw_term_slot(key, part):
    key = jax.random.fold_in(key, 7)
    slots = N_SECTOR * CAP
    per_device = OB * CH_DEV * TPC

    def one_device(device_key):
        first_key, second_key, third_key = jax.random.split(device_key, 3)
        covered = jax.random.permutation(first_key, slots).astype(jnp.int32)
        extra = jax.random.randint(second_key, (per_device - slots,), 0, slots, dtype=jnp.int32)
        return jax.random.permutation(third_key, jnp.concatenate([covered, extra]))
    device_keys = jax.random.split(key, N_SECTOR * N_CHAN)
    values = jax.vmap(one_device)(device_keys).reshape(N_SECTOR, N_CHAN, OB, CH_DEV, TPC)
    return values.transpose(0, 2, 1, 3, 4).reshape(NBLK, CH, TPC).astype(jnp.int32)


def touch_ends(result, rng, smallest, high):
    longest = result.shape.index(max(result.shape))
    spots = []
    for shift in (0, 1):
        where = [jax.random.randint(jax.random.fold_in(rng, axis), (), 0, length) for axis, length in enumerate(result.shape)]
        where[longest] = (where[longest] + shift) % result.shape[longest]
        spots.append(tuple(where))
    return result.at[spots[0]].set(smallest).at[spots[1]].set(high)


def block_scale(key, shape, pieces, least, high):
    def one(position, parts):
        heights = jax.random.uniform(jax.random.fold_in(jax.random.fold_in(key, 6), position), (parts,), jnp.float32, least / len(pieces), high / len(pieces))
        return jnp.repeat(jnp.exp(heights), shape[position] // parts).reshape((-1,) + (1,) * (len(shape) - position - 1))

    gain = one(*pieces[0])
    for cut in pieces[1:]:
        gain = gain * one(*cut)
    return gain


def bell_draw(stream_key, shape, width, most, pieces=(), kind=jnp.bfloat16):
    result = jax.random.normal(stream_key, shape, jnp.float32) * width
    if len(pieces) > 0:
        result = block_scale(stream_key, shape, pieces, -0.22, 0.18) * result
    return jnp.clip(result, min=-most, max=most).astype(kind)


def setup_inputs(seed: int = 0, part: int = 0) -> dict:
    key_list = jax.random.split(jax.random.key(seed), 8)
    part_splits = jax.random.split(jax.random.fold_in(key_list[7], part), 8)
    return {
        "theta": bell_draw(part_splits[0], (NBLK, M, M), 1.0, 6.0, ((0, 4),)),
        "left_env": bell_draw(part_splits[1], (CH, NBLK, M, M), M ** -0.5, 0.375, ((0, 2), (1, 4), (2, 2))),
        "right_env": bell_draw(part_splits[2], (CH, NBLK, M, M), M ** -0.5, 0.375, ((0, 2), (1, 4))),
        "coef": bell_draw(part_splits[3], (NBLK, CH, TPC), 0.1, 0.6, ((0, 4), (1, 2)), jnp.float32),
        "term_slot": draw_term_slot(jax.random.fold_in(jax.random.fold_in(key_list[7], part), 71), part),
        "need": touch_ends(jax.random.randint(part_splits[5], (N_SECTOR, N_SECTOR, CAP), 0, OB), jax.random.fold_in(part_splits[5], 1), 0, OB - 1).astype(jnp.int32),
        "dims": touch_ends(jax.random.randint(part_splits[6], (NBLK, 2), M // 4, M + 1), jax.random.fold_in(part_splits[6], 1), M // 4, M).astype(jnp.int32),
    }


def live_mask(counts, order):
    index = jnp.arange(order, dtype=jnp.int32)
    return (index[None, :, None] < counts[:, 0][:, None, None]) & (index[None, None, :] < counts[:, 1][:, None, None])


def reference(theta, left_env, right_env, coef, term_slot, need, dims):
    order = theta.shape[1]
    masked = jnp.where(live_mask(dims, order), theta, jnp.zeros_like(theta))

    def one_block(block):
        owner = block // OB
        slots = term_slot[block]
        sender = slots // CAP
        local = need[owner, sender, slots % CAP]
        source = jnp.take(masked, (sender * OB + local).astype(jnp.int32), axis=0)
        left = jnp.take(left_env, block, axis=1).astype(jnp.float32)
        right = jnp.take(right_env, block, axis=1).astype(jnp.float32)
        partial_value = jnp.einsum("whm,wkmn->wkhn", left, source.astype(jnp.float32)).astype(jnp.bfloat16)
        image = jnp.einsum("wkhn,wpn->wkhp", partial_value.astype(jnp.float32), right)
        weights = coef[block]
        return jnp.sum(image * weights[:, :, None, None], axis=(0, 1))

    total = lax.map(one_block, jnp.arange(theta.shape[0], dtype=jnp.int32))
    return jnp.where(live_mask(dims, order), total, jnp.zeros_like(total))
```

```python
import functools

import jax
import jax.numpy as jnp
from jax import lax
from jax.experimental import pallas as pl
from jax.experimental.pallas import tpu as pltpu
from jax.sharding import PartitionSpec as P

MESH = pl.DeviceIdType.MESH


def live(block, row_start, rows_live, cols_live):
    row = row_start + lax.broadcasted_iota(jnp.int32, block.shape, 0)
    col = lax.broadcasted_iota(jnp.int32, block.shape, 1)
    keep = jnp.logical_and(row < rows_live, col < cols_live)
    return jnp.where(keep, block, jnp.zeros_like(block))


def kernel(
    n_sector, n_chan, n_rep,
    coef, slots, need, dims, theta_hbm, left_hbm, right_hbm, out_hbm,
    theta, left, right, outgoing, source, totals, result,
    local_sem, out_sem, z_send, z_recv, x_send, x_recv, f_send, f_recv, y_send, y_recv,
):
    channels, blocks, half_rows, order = left.shape
    cap = need.shape[2]
    terms = slots.shape[2]
    me = lax.axis_index("sector")
    chan = lax.axis_index("chan")
    rep = lax.axis_index("rep")
    other = 1 - rep
    piece_rows = order // (n_chan * n_rep)

    theta_copy = pltpu.make_async_copy(theta_hbm, theta, local_sem.at[0])
    left_copy = pltpu.make_async_copy(left_hbm, left, local_sem.at[1])
    right_copy = pltpu.make_async_copy(right_hbm, right, local_sem.at[2])
    theta_copy.start()
    left_copy.start()
    right_copy.start()

    def each_sector(act):
        def step(i, carry):
            s = me + (1 - 2 * (i % 2)) * (i // 2 + 1)

            @pl.when(jnp.logical_and(s >= 0, s < n_sector))
            def _():
                act(s)

            return carry

        lax.fori_loop(0, 2 * (n_sector - 1), step, 0)

    def each_chan(act):
        def step(i, carry):
            act((chan + i) % n_chan)
            return carry

        lax.fori_loop(1, n_chan, step, 0)

    barrier = pltpu.get_barrier_semaphore()
    each_sector(lambda s: pl.semaphore_signal(barrier, 1, device_id={"sector": s}, device_id_type=MESH))
    each_chan(lambda c: pl.semaphore_signal(barrier, 1, device_id={"chan": c}, device_id_type=MESH))
    pl.semaphore_signal(barrier, 1, device_id={"rep": other}, device_id_type=MESH)

    def start_of(c, r):
        return pl.multiple_of((c * n_rep + r) * piece_rows, piece_rows)

    def piece(s, c, r):
        return source.at[pl.ds(s * cap, cap), pl.ds(start_of(c, r), piece_rows), :]

    def z_copy(s, at):
        return pltpu.make_async_remote_copy(
            src_ref=outgoing.at[s], dst_ref=piece(at, chan, rep),
            send_sem=z_send.at[s], recv_sem=z_recv.at[at],
            device_id={"sector": s}, device_id_type=MESH)

    def x_copy(s, c, at):
        return pltpu.make_async_remote_copy(
            src_ref=piece(s, chan, rep), dst_ref=piece(s, at, rep),
            send_sem=x_send.at[s, c], recv_sem=x_recv.at[s, at],
            device_id={"chan": c}, device_id_type=MESH)

    def f_copy(s, c, r):
        return pltpu.make_async_remote_copy(
            src_ref=piece(s, c, rep), dst_ref=piece(s, c, r),
            send_sem=f_send.at[s, c], recv_sem=f_recv.at[s, c],
            device_id={"rep": other}, device_id_type=MESH)

    def y_copy(o, c, at):
        return pltpu.make_async_remote_copy(
            src_ref=totals.at[chan, o], dst_ref=totals.at[at, o],
            send_sem=y_send.at[c, o], recv_sem=y_recv.at[at, o],
            device_id={"chan": c}, device_id_type=MESH)

    theta_copy.wait()
    pl.semaphore_wait(barrier, n_sector - 1 + n_chan - 1 + 1)

    def send_theta(s):
        for c in range(cap):
            b = need[s, me, c]
            first = start_of(chan, rep)
            rows = theta[b, pl.ds(first, piece_rows), :].astype(jnp.float32)
            outgoing[s, c] = live(rows, first, dims[b, 0], dims[b, 1]).astype(jnp.bfloat16)
        z_copy(s, me).start()

    each_sector(send_theta)

    for c in range(cap):
        b = need[me, me, c]
        whole = theta[b].astype(jnp.float32)
        source[me * cap + c] = live(whole, 0, dims[b, 0], dims[b, 1]).astype(jnp.bfloat16)

    def pass_on(s):
        z_copy(s, s).wait_recv()
        each_chan(lambda c: x_copy(s, c, chan).start())
        f_copy(s, chan, rep).start()

    each_sector(pass_on)

    def pass_second(s):
        def one(c):
            x_copy(s, c, c).wait_recv()
            f_copy(s, c, rep).start()

        each_chan(one)

    each_sector(pass_second)
    left_copy.wait()
    right_copy.wait()

    def gather_rest(s):
        f_copy(s, chan, other).wait_recv()
        each_chan(lambda c: f_copy(s, c, other).wait_recv())

    each_sector(gather_rest)

    def block_product(o, carry):
        total = jnp.zeros((half_rows, order), jnp.float32)
        for w in range(channels):
            mixed = jnp.zeros((half_rows, order), jnp.float32)
            for k in range(terms):
                partial = jnp.dot(
                    left[w, o], source[slots[o, w, k]], preferred_element_type=jnp.float32
                ).astype(jnp.bfloat16)
                mixed = mixed + coef[o, w, k] * partial.astype(jnp.float32)
            high = mixed.astype(jnp.bfloat16)
            low = (mixed - high.astype(jnp.float32)).astype(jnp.bfloat16)
            for part in (high, low):
                total = total + lax.dot_general(
                    part, right[w, o], (((1,), (1,)), ((), ())), preferred_element_type=jnp.float32
                )
        totals[chan, o] = total.astype(jnp.bfloat16)
        each_chan(lambda c: y_copy(o, c, chan).start())
        return carry

    lax.fori_loop(0, blocks, block_product, 0)

    def finish(o, carry):
        each_chan(lambda c: y_copy(o, c, c).wait_recv())
        total = totals[0, o].astype(jnp.float32)
        for c in range(1, n_chan):
            total = total + totals[c, o].astype(jnp.float32)
        result[o] = live(total, rep * half_rows, dims[o, 0], dims[o, 1])
        pltpu.make_async_copy(result.at[o], out_hbm.at[o], out_sem.at[o]).start()
        return carry

    lax.fori_loop(0, blocks, finish, 0)

    def drain_theta(s):
        z_copy(s, me).wait_send()
        each_chan(lambda c: x_copy(s, c, chan).wait_send())
        f_copy(s, chan, rep).wait_send()
        each_chan(lambda c: f_copy(s, c, rep).wait_send())

    each_sector(drain_theta)

    def drain(o, carry):
        each_chan(lambda c: y_copy(o, c, chan).wait_send())
        pltpu.make_async_copy(result.at[o], out_hbm.at[o], out_sem.at[o]).wait()
        return carry

    lax.fori_loop(0, blocks, drain, 0)


def body(n_sector, n_chan, n_rep, theta, left_env, right_env, coef, term_slot, need, dims):
    blocks, order, _ = theta.shape
    channels, _, half_rows, _ = left_env.shape
    cap = need.shape[2]
    dma = pltpu.SemaphoreType.DMA
    smem = pl.BlockSpec(memory_space=pltpu.SMEM)
    hbm = pl.BlockSpec(memory_space=pl.ANY)
    flops = 2 * blocks * channels * (term_slot.shape[2] + 2) * half_rows * order * order
    return pl.pallas_call(
        functools.partial(kernel, n_sector, n_chan, n_rep),
        out_shape=jax.ShapeDtypeStruct((blocks, half_rows, order), jnp.float32),
        in_specs=[smem] * 4 + [hbm] * 3,
        out_specs=hbm,
        scratch_shapes=[
            pltpu.VMEM(theta.shape, jnp.bfloat16),
            pltpu.VMEM(left_env.shape, jnp.bfloat16),
            pltpu.VMEM(right_env.shape, jnp.bfloat16),
            pltpu.VMEM((n_sector, cap, order // (n_chan * n_rep), order), jnp.bfloat16),
            pltpu.VMEM((n_sector * cap, order, order), jnp.bfloat16),
            pltpu.VMEM((n_chan, blocks, half_rows, order), jnp.bfloat16),
            pltpu.VMEM((blocks, half_rows, order), jnp.float32),
            dma((3,)),
            dma((blocks,)),
            dma((n_sector,)),
            dma((n_sector,)),
            dma((n_sector, n_chan)),
            dma((n_sector, n_chan)),
            dma((n_sector, n_chan)),
            dma((n_sector, n_chan)),
            dma((n_chan, blocks)),
            dma((n_chan, blocks)),
        ],
        compiler_params=pltpu.CompilerParams(
            collective_id=0, has_side_effects=True, vmem_limit_bytes=40 * 1024 * 1024
        ),
        cost_estimate=pl.CostEstimate(flops=flops, bytes_accessed=6 * 1024 * 1024, transcendentals=0),
        name="product",
    )(coef, term_slot, need, dims, theta, left_env, right_env)


def solution(mesh):
    in_specs = (
        P(("groups", "sector"), None, None),
        P(("groups", "chan"), "sector", "rep", None),
        P(("groups", "chan"), "sector", None, None),
        P(("groups", "sector"), "chan", None),
        P(("groups", "sector"), "chan", None),
        P("groups", None, None),
        P(("groups", "sector"), None),
    )
    out_specs = P(("groups", "sector"), "rep", None)
    sizes = mesh.shape
    local = functools.partial(body, sizes["sector"], sizes["chan"], sizes["rep"])
    return jax.shard_map(local, mesh=mesh, in_specs=in_specs, out_specs=out_specs, check_vma=False)
```

```python
import functools

import jax
import jax.numpy as jnp
from jax import lax
from jax.experimental import pallas as pl
from jax.experimental.pallas import tpu as pltpu
from jax.sharding import PartitionSpec as P

MESH = pl.DeviceIdType.MESH


def live(block, row_start, rows_live, cols_live):
    row = row_start + lax.broadcasted_iota(jnp.int32, block.shape, 0)
    col = lax.broadcasted_iota(jnp.int32, block.shape, 1)
    keep = jnp.logical_and(row < rows_live, col < cols_live)
    return jnp.where(keep, block, jnp.zeros_like(block))


def shared_rows(half_rows, n_chan):
    return 16 * max(1, half_rows // (2 * 16 * n_chan))


def kernel(
    n_sector, n_chan, n_rep,
    coef, slots, need, dims, theta_hbm, left_hbm, right_hbm, out_hbm,
    theta, left, right, outgoing, source, totals,
    local_sem, out_sem, z_send, z_recv, x_send, x_recv, d_send, d_recv, f_send, f_recv, y_send, y_recv,
):
    channels, blocks, half_rows, order = left.shape
    cap = need.shape[1]
    terms = slots.shape[1]
    me = lax.axis_index("sector")
    chan = lax.axis_index("chan")
    rep = lax.axis_index("rep")
    other = 1 - rep
    piece_rows = shared_rows(half_rows, n_chan)
    direct_rows = half_rows - piece_rows * n_chan

    theta_copy = pltpu.make_async_copy(theta_hbm, theta, local_sem.at[0])
    left_copy = pltpu.make_async_copy(left_hbm, left, local_sem.at[1])
    right_copy = pltpu.make_async_copy(right_hbm, right, local_sem.at[2])
    theta_copy.start()
    left_copy.start()
    right_copy.start()

    def each_sector(act):
        for d in range(1, n_sector):
            act((me + d) % n_sector)

    def each_chan(act):
        for d in range(1, n_chan):
            act((chan + d) % n_chan)

    barrier = pltpu.get_barrier_semaphore()
    each_sector(lambda s: pl.semaphore_signal(barrier, 1, device_id={"sector": s}, device_id_type=MESH))
    each_chan(lambda c: pl.semaphore_signal(barrier, 1, device_id={"chan": c}, device_id_type=MESH))
    pl.semaphore_signal(barrier, 1, device_id={"rep": other}, device_id_type=MESH)

    def start_of(c, r):
        return pl.multiple_of(r * half_rows + c * piece_rows, 16)

    def piece(s, c, r):
        rows = direct_rows if isinstance(c, int) and c == n_chan else piece_rows
        return source.at[pl.ds(s * cap, cap), pl.ds(start_of(c, r), rows), :]

    def z_copy(s, at):
        return pltpu.make_async_remote_copy(
            src_ref=outgoing.at[s, :, pl.ds(0, piece_rows), :], dst_ref=piece(at, chan, rep),
            send_sem=z_send.at[s], recv_sem=z_recv.at[at],
            device_id={"sector": s}, device_id_type=MESH)

    def d_copy(s, at):
        return pltpu.make_async_remote_copy(
            src_ref=outgoing.at[s, :, pl.ds(piece_rows, direct_rows), :], dst_ref=piece(at, n_chan, rep),
            send_sem=d_send.at[s], recv_sem=d_recv.at[at],
            device_id={"sector": s}, device_id_type=MESH)

    def x_copy(s, c, at):
        return pltpu.make_async_remote_copy(
            src_ref=piece(s, chan, rep), dst_ref=piece(s, at, rep),
            send_sem=x_send.at[s, c], recv_sem=x_recv.at[s, at],
            device_id={"chan": c}, device_id_type=MESH)

    def f_copy(s, c, r):
        return pltpu.make_async_remote_copy(
            src_ref=piece(s, c, rep), dst_ref=piece(s, c, r),
            send_sem=f_send.at[s, c], recv_sem=f_recv.at[s, c],
            device_id={"rep": other}, device_id_type=MESH)

    def y_copy(o, c, at):
        return pltpu.make_async_remote_copy(
            src_ref=totals.at[o], dst_ref=out_hbm.at[at, o],
            send_sem=y_send.at[c, o], recv_sem=y_recv.at[at, o],
            device_id={"chan": c}, device_id_type=MESH)

    theta_copy.wait()
    def prepare(s):
        for k in range(cap):
            b = need[s, k, me]
            for c, at, rows in ((chan, 0, piece_rows), (n_chan, piece_rows, direct_rows)):
                if rows:
                    first = start_of(c, rep)
                    part = theta[b, pl.ds(first, rows), :].astype(jnp.float32)
                    part = live(part, first, dims[0, b], dims[1, b]).astype(jnp.bfloat16)
                    outgoing[s, k, pl.ds(at, rows), :] = part

    each_sector(prepare)
    for c in range(cap):
        b = need[me, c, me]
        whole = theta[b].astype(jnp.float32)
        source[me * cap + c] = live(whole, 0, dims[0, b], dims[1, b]).astype(jnp.bfloat16)

    pl.semaphore_wait(barrier, n_sector - 1 + n_chan - 1 + 1)

    each_sector(lambda s: z_copy(s, me).start())

    def pass_on(s):
        z_copy(s, s).wait_recv()
        each_chan(lambda c: x_copy(s, c, chan).start())
        f_copy(s, chan, rep).start()

    if direct_rows:
        each_sector(lambda s: d_copy(s, me).start())
    each_sector(pass_on)

    def pass_second(s):
        def one(c):
            x_copy(s, c, c).wait_recv()
            f_copy(s, c, rep).start()

        each_chan(one)

    each_sector(pass_second)

    def pass_direct(s):
        d_copy(s, s).wait_recv()
        f_copy(s, n_chan, rep).start()

    if direct_rows:
        each_sector(pass_direct)
    left_copy.wait()
    right_copy.wait()

    def gather_rest(s):
        f_copy(s, chan, other).wait_recv()
        each_chan(lambda c: f_copy(s, c, other).wait_recv())
        if direct_rows:
            f_copy(s, n_chan, other).wait_recv()

    each_sector(gather_rest)

    def own_copy(o):
        return pltpu.make_async_copy(totals.at[o], out_hbm.at[chan, o], out_sem.at[o])

    def block_product(o, carry):
        total = jnp.zeros((half_rows, order), jnp.float32)
        for w in range(channels):
            mixed = jnp.zeros((half_rows, order), jnp.float32)
            for k in range(terms):
                partial = jnp.dot(
                    left[w, o], source[slots[w, k, o]], preferred_element_type=jnp.float32
                ).astype(jnp.bfloat16)
                mixed = mixed + coef[w, k, o] * partial.astype(jnp.float32)
            high = mixed.astype(jnp.bfloat16)
            low = (mixed - high.astype(jnp.float32)).astype(jnp.bfloat16)
            for part in (high, low):
                total = total + lax.dot_general(
                    part, right[w, o], (((1,), (1,)), ((), ())), preferred_element_type=jnp.float32
                )
        totals[o] = live(total, rep * half_rows, dims[0, o], dims[1, o]).astype(jnp.bfloat16)
        each_chan(lambda c: y_copy(o, c, chan).start())
        own_copy(o).start()
        return carry

    lax.fori_loop(0, blocks, block_product, 0)

    def finish(o, carry):
        each_chan(lambda c: y_copy(o, c, c).wait_recv())
        return carry

    lax.fori_loop(0, blocks, finish, 0)

    def drain_theta(s):
        z_copy(s, me).wait_send()
        each_chan(lambda c: x_copy(s, c, chan).wait_send())
        f_copy(s, chan, rep).wait_send()
        each_chan(lambda c: f_copy(s, c, rep).wait_send())
        if direct_rows:
            d_copy(s, me).wait_send()
            f_copy(s, n_chan, rep).wait_send()

    each_sector(drain_theta)

    def drain(o, carry):
        each_chan(lambda c: y_copy(o, c, chan).wait_send())
        own_copy(o).wait()
        return carry

    lax.fori_loop(0, blocks, drain, 0)


def body(n_sector, n_chan, n_rep, theta, left_env, right_env, coef, term_slot, need, dims):
    blocks, order, _ = theta.shape
    channels, _, half_rows, _ = left_env.shape
    cap = need.shape[2]
    dma = pltpu.SemaphoreType.DMA
    rows_out = half_rows - (n_chan - 1) * shared_rows(half_rows, n_chan)
    smem = pl.BlockSpec(memory_space=pltpu.SMEM)
    hbm = pl.BlockSpec(memory_space=pl.ANY)
    flops = 2 * blocks * channels * (term_slot.shape[2] + 2) * half_rows * order * order
    totals = pl.pallas_call(
        functools.partial(kernel, n_sector, n_chan, n_rep),
        out_shape=jax.ShapeDtypeStruct((n_chan, blocks, half_rows, order), jnp.bfloat16),
        in_specs=[smem] * 4 + [hbm] * 3,
        out_specs=hbm,
        scratch_shapes=[
            pltpu.VMEM(theta.shape, jnp.bfloat16),
            pltpu.VMEM(left_env.shape, jnp.bfloat16),
            pltpu.VMEM(right_env.shape, jnp.bfloat16),
            pltpu.VMEM((n_sector, cap, rows_out, order), jnp.bfloat16),
            pltpu.VMEM((n_sector * cap, order, order), jnp.bfloat16),
            pltpu.VMEM((blocks, half_rows, order), jnp.bfloat16),
            dma((3,)),
            dma((blocks,)),
            dma((n_sector,)),
            dma((n_sector,)),
            dma((n_sector, n_chan)),
            dma((n_sector, n_chan)),
            dma((n_sector,)),
            dma((n_sector,)),
            dma((n_sector, n_chan + 1)),
            dma((n_sector, n_chan + 1)),
            dma((n_chan, blocks)),
            dma((n_chan, blocks)),
        ],
        compiler_params=pltpu.CompilerParams(
            collective_id=0, has_side_effects=True, vmem_limit_bytes=60 * 1024 * 1024
        ),
        cost_estimate=pl.CostEstimate(flops=flops, bytes_accessed=6 * 1024 * 1024, transcendentals=0),
        name="product",
    )(
        coef.transpose(1, 2, 0), term_slot.transpose(1, 2, 0), need.transpose(0, 2, 1), dims.T,
        theta, left_env, right_env,
    )
    total = totals[0].astype(jnp.float32)
    for c in range(1, n_chan):
        total = total + totals[c].astype(jnp.float32)
    return total


def solution(mesh):
    in_specs = (
        P(("groups", "sector"), None, None),
        P(("groups", "chan"), "sector", "rep", None),
        P(("groups", "chan"), "sector", None, None),
        P(("groups", "sector"), "chan", None),
        P(("groups", "sector"), "chan", None),
        P("groups", None, None),
        P(("groups", "sector"), None),
    )
    out_specs = P(("groups", "sector"), "rep", None)
    sizes = mesh.shape
    local = functools.partial(body, sizes["sector"], sizes["chan"], sizes["rep"])
    return jax.shard_map(local, mesh=mesh, in_specs=in_specs, out_specs=out_specs, check_vma=False)
```

```python
import functools

import jax
import jax.numpy as jnp
from jax import lax
from jax.experimental import pallas as pl
from jax.experimental.pallas import tpu as pltpu
from jax.sharding import PartitionSpec as P

MESH = pl.DeviceIdType.MESH


def live(block, row_start, rows_live, cols_live):
    row = row_start + lax.broadcasted_iota(jnp.int32, block.shape, 0)
    col = lax.broadcasted_iota(jnp.int32, block.shape, 1)
    keep = jnp.logical_and(row < rows_live, col < cols_live)
    return jnp.where(keep, block, jnp.zeros_like(block))


def shared_rows(half_rows, n_chan):
    return 16 * max(1, half_rows // (2 * 16 * n_chan))


def kernel(
    n_sector, n_chan, n_rep,
    coef, slots, need, dims, theta_hbm, left_hbm, right_hbm, out_hbm,
    theta, left, right, outgoing, source, totals,
    local_sem, out_sem, z_send, z_recv, x_send, x_recv, d_send, d_recv, f_send, f_recv, y_send, y_recv,
):
    channels, blocks, half_rows, order = left.shape
    cap = need.shape[1]
    terms = slots.shape[1]
    me = lax.axis_index("sector")
    chan = lax.axis_index("chan")
    rep = lax.axis_index("rep")
    other = 1 - rep
    piece_rows = shared_rows(half_rows, n_chan)
    direct_rows = half_rows - piece_rows * n_chan

    theta_copy = pltpu.make_async_copy(theta_hbm, theta, local_sem.at[0])
    left_copy = pltpu.make_async_copy(left_hbm, left, local_sem.at[1])
    right_copy = pltpu.make_async_copy(right_hbm, right, local_sem.at[2])
    theta_copy.start()
    left_copy.start()
    right_copy.start()

    def each_sector(act):
        for d in range(1, n_sector):
            act((me + d) % n_sector)

    def each_chan(act):
        for d in range(1, n_chan):
            act((chan + d) % n_chan)

    barrier = pltpu.get_barrier_semaphore()
    each_sector(lambda s: pl.semaphore_signal(barrier, 1, device_id={"sector": s}, device_id_type=MESH))
    each_chan(lambda c: pl.semaphore_signal(barrier, 1, device_id={"chan": c}, device_id_type=MESH))
    pl.semaphore_signal(barrier, 1, device_id={"rep": other}, device_id_type=MESH)

    def start_of(c, r):
        return pl.multiple_of(r * half_rows + c * piece_rows, 16)

    def piece(s, c, r):
        rows = direct_rows if isinstance(c, int) and c == n_chan else piece_rows
        return source.at[pl.ds(s * cap, cap), pl.ds(start_of(c, r), rows), :]

    def z_copy(s, at):
        return pltpu.make_async_remote_copy(
            src_ref=outgoing.at[s, :, pl.ds(0, piece_rows), :], dst_ref=piece(at, chan, rep),
            send_sem=z_send.at[s], recv_sem=z_recv.at[at],
            device_id={"sector": s}, device_id_type=MESH)

    def d_copy(s, at):
        return pltpu.make_async_remote_copy(
            src_ref=outgoing.at[s, :, pl.ds(piece_rows, direct_rows), :], dst_ref=piece(at, n_chan, rep),
            send_sem=d_send.at[s], recv_sem=d_recv.at[at],
            device_id={"sector": s}, device_id_type=MESH)

    def x_copy(s, c, at):
        return pltpu.make_async_remote_copy(
            src_ref=piece(s, chan, rep), dst_ref=piece(s, at, rep),
            send_sem=x_send.at[s, c], recv_sem=x_recv.at[s, at],
            device_id={"chan": c}, device_id_type=MESH)

    def f_copy(s, c, r):
        return pltpu.make_async_remote_copy(
            src_ref=piece(s, c, rep), dst_ref=piece(s, c, r),
            send_sem=f_send.at[s, c], recv_sem=f_recv.at[s, c],
            device_id={"rep": other}, device_id_type=MESH)

    def y_copy(o, c, at):
        return pltpu.make_async_remote_copy(
            src_ref=totals.at[o], dst_ref=out_hbm.at[at, o],
            send_sem=y_send.at[c, o], recv_sem=y_recv.at[at, o],
            device_id={"chan": c}, device_id_type=MESH)

    theta_copy.wait()
    def prepare(s):
        for k in range(cap):
            b = need[s, k, me]
            for c, at, rows in ((chan, 0, piece_rows), (n_chan, piece_rows, direct_rows)):
                if rows:
                    first = start_of(c, rep)
                    part = theta[b, pl.ds(first, rows), :].astype(jnp.float32)
                    part = live(part, first, dims[0, b], dims[1, b]).astype(jnp.bfloat16)
                    outgoing[s, k, pl.ds(at, rows), :] = part

    each_sector(prepare)
    for c in range(cap):
        b = need[me, c, me]
        whole = theta[b].astype(jnp.float32)
        source[me * cap + c] = live(whole, 0, dims[0, b], dims[1, b]).astype(jnp.bfloat16)

    pl.semaphore_wait(barrier, n_sector - 1 + n_chan - 1 + 1)

    each_sector(lambda s: z_copy(s, me).start())

    def pass_on(s):
        z_copy(s, s).wait_recv()
        each_chan(lambda c: x_copy(s, c, chan).start())
        f_copy(s, chan, rep).start()

    if direct_rows:
        each_sector(lambda s: d_copy(s, me).start())
    each_sector(pass_on)

    def pass_second(s):
        def one(c):
            x_copy(s, c, c).wait_recv()
            f_copy(s, c, rep).start()

        each_chan(one)

    each_sector(pass_second)

    def pass_direct(s):
        d_copy(s, s).wait_recv()
        f_copy(s, n_chan, rep).start()

    if direct_rows:
        each_sector(pass_direct)
    left_copy.wait()
    right_copy.wait()

    def gather_rest(s):
        f_copy(s, chan, other).wait_recv()
        each_chan(lambda c: f_copy(s, c, other).wait_recv())
        if direct_rows:
            f_copy(s, n_chan, other).wait_recv()

    each_sector(gather_rest)

    def own_copy(o):
        return pltpu.make_async_copy(totals.at[o], out_hbm.at[chan, o], out_sem.at[o])

    def block_product(o, carry):
        total = jnp.zeros((half_rows, order), jnp.float32)
        for w in range(channels):
            mixed = jnp.zeros((half_rows, order), jnp.float32)
            for k in range(terms):
                partial = jnp.dot(
                    left[w, o], source[slots[w, k, o]], preferred_element_type=jnp.float32
                ).astype(jnp.bfloat16)
                mixed = mixed + coef[w, k, o] * partial.astype(jnp.float32)
            high = mixed.astype(jnp.bfloat16)
            low = (mixed - high.astype(jnp.float32)).astype(jnp.bfloat16)
            image = lax.dot_general(
                jnp.concatenate([high, low], axis=0), right[w, o],
                (((1,), (1,)), ((), ())), preferred_element_type=jnp.float32,
            )
            total = total + (image[:half_rows] + image[half_rows:])
        totals[o] = live(total, rep * half_rows, dims[0, o], dims[1, o]).astype(jnp.bfloat16)
        each_chan(lambda c: y_copy(o, c, chan).start())
        own_copy(o).start()
        return carry

    lax.fori_loop(0, blocks, block_product, 0)

    def finish(o, carry):
        each_chan(lambda c: y_copy(o, c, c).wait_recv())
        return carry

    lax.fori_loop(0, blocks, finish, 0)

    def drain_theta(s):
        z_copy(s, me).wait_send()
        each_chan(lambda c: x_copy(s, c, chan).wait_send())
        f_copy(s, chan, rep).wait_send()
        each_chan(lambda c: f_copy(s, c, rep).wait_send())
        if direct_rows:
            d_copy(s, me).wait_send()
            f_copy(s, n_chan, rep).wait_send()

    each_sector(drain_theta)

    def drain(o, carry):
        each_chan(lambda c: y_copy(o, c, chan).wait_send())
        own_copy(o).wait()
        return carry

    lax.fori_loop(0, blocks, drain, 0)


def body(n_sector, n_chan, n_rep, theta, left_env, right_env, coef, term_slot, need, dims):
    blocks, order, _ = theta.shape
    channels, _, half_rows, _ = left_env.shape
    cap = need.shape[2]
    dma = pltpu.SemaphoreType.DMA
    rows_out = half_rows - (n_chan - 1) * shared_rows(half_rows, n_chan)
    smem = pl.BlockSpec(memory_space=pltpu.SMEM)
    hbm = pl.BlockSpec(memory_space=pl.ANY)
    flops = 2 * blocks * channels * (term_slot.shape[2] + 2) * half_rows * order * order
    totals = pl.pallas_call(
        functools.partial(kernel, n_sector, n_chan, n_rep),
        out_shape=jax.ShapeDtypeStruct((n_chan, blocks, half_rows, order), jnp.bfloat16),
        in_specs=[smem] * 4 + [hbm] * 3,
        out_specs=hbm,
        scratch_shapes=[
            pltpu.VMEM(theta.shape, jnp.bfloat16),
            pltpu.VMEM(left_env.shape, jnp.bfloat16),
            pltpu.VMEM(right_env.shape, jnp.bfloat16),
            pltpu.VMEM((n_sector, cap, rows_out, order), jnp.bfloat16),
            pltpu.VMEM((n_sector * cap, order, order), jnp.bfloat16),
            pltpu.VMEM((blocks, half_rows, order), jnp.bfloat16),
            dma((3,)),
            dma((blocks,)),
            dma((n_sector,)),
            dma((n_sector,)),
            dma((n_sector, n_chan)),
            dma((n_sector, n_chan)),
            dma((n_sector,)),
            dma((n_sector,)),
            dma((n_sector, n_chan + 1)),
            dma((n_sector, n_chan + 1)),
            dma((n_chan, blocks)),
            dma((n_chan, blocks)),
        ],
        compiler_params=pltpu.CompilerParams(
            collective_id=0, has_side_effects=True, vmem_limit_bytes=60 * 1024 * 1024
        ),
        cost_estimate=pl.CostEstimate(flops=flops, bytes_accessed=6 * 1024 * 1024, transcendentals=0),
        name="product",
    )(
        coef.transpose(1, 2, 0), term_slot.transpose(1, 2, 0), need.transpose(0, 2, 1), dims.T,
        theta, left_env, right_env,
    )
    total = totals[0].astype(jnp.float32)
    for c in range(1, n_chan):
        total = total + totals[c].astype(jnp.float32)
    return total


def solution(mesh):
    in_specs = (
        P(("groups", "sector"), None, None),
        P(("groups", "chan"), "sector", "rep", None),
        P(("groups", "chan"), "sector", None, None),
        P(("groups", "sector"), "chan", None),
        P(("groups", "sector"), "chan", None),
        P("groups", None, None),
        P(("groups", "sector"), None),
    )
    out_specs = P(("groups", "sector"), "rep", None)
    sizes = mesh.shape
    local = functools.partial(body, sizes["sector"], sizes["chan"], sizes["rep"])
    return jax.shard_map(local, mesh=mesh, in_specs=in_specs, out_specs=out_specs, check_vma=False)
```

```python
import functools

import jax
import jax.numpy as jnp
from jax import lax
from jax.experimental import pallas as pl
from jax.experimental.pallas import tpu as pltpu
from jax.sharding import PartitionSpec as P

MESH = pl.DeviceIdType.MESH


def live(block, row_start, rows_live, cols_live):
    row = row_start + lax.broadcasted_iota(jnp.int32, block.shape, 0)
    col = lax.broadcasted_iota(jnp.int32, block.shape, 1)
    keep = jnp.logical_and(row < rows_live, col < cols_live)
    return jnp.where(keep, block, jnp.zeros_like(block))


def shared_rows(half_rows, n_chan):
    return 16 * max(1, half_rows // (2 * 16 * n_chan))


def add_shards(totals, out):
    total = totals[0].astype(jnp.float32)
    for c in range(1, totals.shape[0]):
        total = total + totals[c].astype(jnp.float32)
    out[...] = total


def kernel(
    n_sector, n_chan, n_rep,
    coef, slots, need, dims, theta_hbm, left_hbm, right_hbm, out_hbm,
    theta, left, right, outgoing, source, totals,
    local_sem, out_sem, z_send, z_recv, x_send, x_recv, d_send, d_recv, f_send, f_recv, y_send, y_recv,
):
    channels, blocks, half_rows, order = left.shape
    cap = need.shape[1]
    terms = slots.shape[1]
    me = lax.axis_index("sector")
    chan = lax.axis_index("chan")
    rep = lax.axis_index("rep")
    other = 1 - rep
    piece_rows = shared_rows(half_rows, n_chan)
    direct_rows = half_rows - piece_rows * n_chan

    theta_copy = pltpu.make_async_copy(theta_hbm, theta, local_sem.at[0])
    left_copy = pltpu.make_async_copy(left_hbm, left, local_sem.at[1])
    right_copy = pltpu.make_async_copy(right_hbm, right, local_sem.at[2])
    theta_copy.start()
    left_copy.start()
    right_copy.start()

    def each_sector(act):
        for d in range(1, n_sector):
            act((me + d) % n_sector)

    def each_chan(act):
        for d in range(1, n_chan):
            act((chan + d) % n_chan)

    barrier = pltpu.get_barrier_semaphore()
    each_sector(lambda s: pl.semaphore_signal(barrier, 1, device_id={"sector": s}, device_id_type=MESH))
    each_chan(lambda c: pl.semaphore_signal(barrier, 1, device_id={"chan": c}, device_id_type=MESH))
    pl.semaphore_signal(barrier, 1, device_id={"rep": other}, device_id_type=MESH)

    def start_of(c, r):
        return pl.multiple_of(r * half_rows + c * piece_rows, 16)

    def piece(s, c, r):
        rows = direct_rows if isinstance(c, int) and c == n_chan else piece_rows
        return source.at[pl.ds(s * cap, cap), pl.ds(start_of(c, r), rows), :]

    def z_copy(s, at):
        return pltpu.make_async_remote_copy(
            src_ref=outgoing.at[s, :, pl.ds(0, piece_rows), :], dst_ref=piece(at, chan, rep),
            send_sem=z_send.at[s], recv_sem=z_recv.at[at],
            device_id={"sector": s}, device_id_type=MESH)

    def d_copy(s, at):
        return pltpu.make_async_remote_copy(
            src_ref=outgoing.at[s, :, pl.ds(piece_rows, direct_rows), :], dst_ref=piece(at, n_chan, rep),
            send_sem=d_send.at[s], recv_sem=d_recv.at[at],
            device_id={"sector": s}, device_id_type=MESH)

    def x_copy(s, c, at):
        return pltpu.make_async_remote_copy(
            src_ref=piece(s, chan, rep), dst_ref=piece(s, at, rep),
            send_sem=x_send.at[s, c], recv_sem=x_recv.at[s, at],
            device_id={"chan": c}, device_id_type=MESH)

    def f_copy(s, c, r):
        return pltpu.make_async_remote_copy(
            src_ref=piece(s, c, rep), dst_ref=piece(s, c, r),
            send_sem=f_send.at[s, c], recv_sem=f_recv.at[s, c],
            device_id={"rep": other}, device_id_type=MESH)

    def y_copy(o, c, at):
        return pltpu.make_async_remote_copy(
            src_ref=totals.at[o], dst_ref=out_hbm.at[at, o],
            send_sem=y_send.at[c, o], recv_sem=y_recv.at[at, o],
            device_id={"chan": c}, device_id_type=MESH)

    theta_copy.wait()
    def prepare(s):
        for k in range(cap):
            b = need[s, k, me]
            for c, at, rows in ((chan, 0, piece_rows), (n_chan, piece_rows, direct_rows)):
                if rows:
                    first = start_of(c, rep)
                    part = theta[b, pl.ds(first, rows), :].astype(jnp.float32)
                    part = live(part, first, dims[0, b], dims[1, b]).astype(jnp.bfloat16)
                    outgoing[s, k, pl.ds(at, rows), :] = part

    each_sector(prepare)
    for c in range(cap):
        b = need[me, c, me]
        whole = theta[b].astype(jnp.float32)
        source[me * cap + c] = live(whole, 0, dims[0, b], dims[1, b]).astype(jnp.bfloat16)

    pl.semaphore_wait(barrier, n_sector - 1 + n_chan - 1 + 1)

    each_sector(lambda s: z_copy(s, me).start())

    def pass_on(s):
        z_copy(s, s).wait_recv()
        each_chan(lambda c: x_copy(s, c, chan).start())
        f_copy(s, chan, rep).start()

    if direct_rows:
        each_sector(lambda s: d_copy(s, me).start())
    each_sector(pass_on)

    def pass_second(s):
        def one(c):
            x_copy(s, c, c).wait_recv()
            f_copy(s, c, rep).start()

        each_chan(one)

    each_sector(pass_second)

    def pass_direct(s):
        d_copy(s, s).wait_recv()
        f_copy(s, n_chan, rep).start()

    if direct_rows:
        each_sector(pass_direct)
    left_copy.wait()
    right_copy.wait()

    def gather_rest(s):
        f_copy(s, chan, other).wait_recv()
        each_chan(lambda c: f_copy(s, c, other).wait_recv())
        if direct_rows:
            f_copy(s, n_chan, other).wait_recv()

    each_sector(gather_rest)

    def own_copy(o):
        return pltpu.make_async_copy(totals.at[o], out_hbm.at[chan, o], out_sem.at[o])

    def block_product(o, carry):
        total = jnp.zeros((half_rows, order), jnp.float32)
        for w in range(channels):
            mixed = jnp.zeros((half_rows, order), jnp.float32)
            for k in range(terms):
                partial = jnp.dot(
                    left[w, o], source[slots[w, k, o]], preferred_element_type=jnp.float32
                ).astype(jnp.bfloat16)
                mixed = mixed + coef[w, k, o] * partial.astype(jnp.float32)
            high = mixed.astype(jnp.bfloat16)
            low = (mixed - high.astype(jnp.float32)).astype(jnp.bfloat16)
            image = lax.dot_general(
                jnp.concatenate([high, low], axis=0), right[w, o],
                (((1,), (1,)), ((), ())), preferred_element_type=jnp.float32,
            )
            total = total + (image[:half_rows] + image[half_rows:])
        totals[o] = live(total, rep * half_rows, dims[0, o], dims[1, o]).astype(jnp.bfloat16)
        each_chan(lambda c: y_copy(o, c, chan).start())
        own_copy(o).start()
        return carry

    lax.fori_loop(0, blocks, block_product, 0)

    def finish(o, carry):
        each_chan(lambda c: y_copy(o, c, c).wait_recv())
        return carry

    lax.fori_loop(0, blocks, finish, 0)

    def drain_theta(s):
        z_copy(s, me).wait_send()
        each_chan(lambda c: x_copy(s, c, chan).wait_send())
        f_copy(s, chan, rep).wait_send()
        each_chan(lambda c: f_copy(s, c, rep).wait_send())
        if direct_rows:
            d_copy(s, me).wait_send()
            f_copy(s, n_chan, rep).wait_send()

    each_sector(drain_theta)

    def drain(o, carry):
        each_chan(lambda c: y_copy(o, c, chan).wait_send())
        own_copy(o).wait()
        return carry

    lax.fori_loop(0, blocks, drain, 0)


def body(n_sector, n_chan, n_rep, theta, left_env, right_env, coef, term_slot, need, dims):
    blocks, order, _ = theta.shape
    channels, _, half_rows, _ = left_env.shape
    cap = need.shape[2]
    dma = pltpu.SemaphoreType.DMA
    rows_out = half_rows - (n_chan - 1) * shared_rows(half_rows, n_chan)
    smem = pl.BlockSpec(memory_space=pltpu.SMEM)
    hbm = pl.BlockSpec(memory_space=pl.ANY)
    flops = 2 * blocks * channels * (term_slot.shape[2] + 2) * half_rows * order * order
    totals = pl.pallas_call(
        functools.partial(kernel, n_sector, n_chan, n_rep),
        out_shape=jax.ShapeDtypeStruct((n_chan, blocks, half_rows, order), jnp.bfloat16),
        in_specs=[smem] * 4 + [hbm] * 3,
        out_specs=hbm,
        scratch_shapes=[
            pltpu.VMEM(theta.shape, jnp.bfloat16),
            pltpu.VMEM(left_env.shape, jnp.bfloat16),
            pltpu.VMEM(right_env.shape, jnp.bfloat16),
            pltpu.VMEM((n_sector, cap, rows_out, order), jnp.bfloat16),
            pltpu.VMEM((n_sector * cap, order, order), jnp.bfloat16),
            pltpu.VMEM((blocks, half_rows, order), jnp.bfloat16),
            dma((3,)),
            dma((blocks,)),
            dma((n_sector,)),
            dma((n_sector,)),
            dma((n_sector, n_chan)),
            dma((n_sector, n_chan)),
            dma((n_sector,)),
            dma((n_sector,)),
            dma((n_sector, n_chan + 1)),
            dma((n_sector, n_chan + 1)),
            dma((n_chan, blocks)),
            dma((n_chan, blocks)),
        ],
        compiler_params=pltpu.CompilerParams(
            collective_id=0, has_side_effects=True, vmem_limit_bytes=60 * 1024 * 1024
        ),
        cost_estimate=pl.CostEstimate(flops=flops, bytes_accessed=6 * 1024 * 1024, transcendentals=0),
        name="product",
    )(
        coef.transpose(1, 2, 0), term_slot.transpose(1, 2, 0), need.transpose(0, 2, 1), dims.T,
        theta, left_env, right_env,
    )
    step = blocks // 2 if blocks % 2 == 0 else 1
    return pl.pallas_call(
        add_shards,
        out_shape=jax.ShapeDtypeStruct((blocks, half_rows, order), jnp.float32),
        grid=(blocks // step,),
        in_specs=[pl.BlockSpec((n_chan, step, half_rows, order), lambda i: (0, i, 0, 0))],
        out_specs=pl.BlockSpec((step, half_rows, order), lambda i: (i, 0, 0)),
        name="add_shards",
    )(totals)


def solution(mesh):
    in_specs = (
        P(("groups", "sector"), None, None),
        P(("groups", "chan"), "sector", "rep", None),
        P(("groups", "chan"), "sector", None, None),
        P(("groups", "sector"), "chan", None),
        P(("groups", "sector"), "chan", None),
        P("groups", None, None),
        P(("groups", "sector"), None),
    )
    out_specs = P(("groups", "sector"), "rep", None)
    sizes = mesh.shape
    local = functools.partial(body, sizes["sector"], sizes["chan"], sizes["rep"])
    return jax.shard_map(local, mesh=mesh, in_specs=in_specs, out_specs=out_specs, check_vma=False)
```
